256 devices in a mesh: row: 8 (over y, core), col: 16 (over z, x_lo), feat: 2 (over x_hi).
Axes of the slice: x: 4 (x_hi: 2, x_lo: 2; x = x_hi * 2 + x_lo), y: 4, z: 8, core: 2. Of those that a mesh axis runs over, the one named last changes fastest.
Arguments:
- features: bfloat16 [49152, 256], P(('col', 'row')), may hold values from -6 to 6
- weight: bfloat16 [256, 256], P(None, 'feat'), may hold values from -0.375 to 0.375
- bias: float32 [256], P('feat'), may hold values from -3 to 3
- blocks: bfloat16 [8, 16, 192, 128, 128], P('row', 'col'), may hold values from -0.09375 to 0.09375
- coords: int32 [8, 16, 192, 2], P('row', 'col'), may hold values from 0 to 47, as said below
- counts: int32 [8, 16], P('row', 'col'), may hold values from 24 to 192, as said below
- cotangent: bfloat16 [49152, 256], P(('row', 'col'), 'feat'), may hold values from -6 to 6
Outputs:
- outputs: bfloat16 [49152, 256], P(('row', 'col'), 'feat')
- grad_in: bfloat16 [49152, 256], P(('col', 'row', 'feat'))
- grad_w: float32 [256, 256], P(None, 'feat')
- grad_b: float32 [256], P('feat')
The draws below stay inside these ranges and needn't reach their ends.
Inputs may be any that keep to these rules, and one draw needn't show every extreme that they name: coords[..., 0] is below 48 and coords[..., 1] is below 24. `counts`: each tile has between 24 and 192 live slots; some tile has 192, some 192 // 8.
All inputs are finite; a program needn't handle non-finite values.
Results may differ from the reference program's by a relative error of at most 0.007.
Values may be sent and summed in bfloat16 or wider, within the bound.
A program may use at most 128 MiB of HBM per device.

```python
import jax
import jax.numpy as jnp
from jax import lax

BS = 128
F = 256
FO = 256
CB = 24
KMAX = 192
RB = 48
NODES = 49152
N_ROW = 8
N_COL = 16


def draw_coords(key, part):
    key = jax.random.fold_in(key, 7)
    first, second = jax.random.split(key)
    row_part = jax.random.randint(first, (N_ROW, N_COL, KMAX, 1), 0, RB)
    col_part = jax.random.randint(second, (N_ROW, N_COL, KMAX, 1), 0, CB)
    return jnp.concatenate([row_part, col_part], axis=3).astype(jnp.int32)


def draw_counts(key, part):
    key = jax.random.fold_in(key, 11)
    first, second = jax.random.split(key)
    shifts = jax.random.randint(first, (N_ROW * N_COL,), 0, 4)
    values = KMAX // jnp.left_shift(jnp.ones_like(shifts), shifts)
    picks = jax.random.permutation(second, N_ROW * N_COL)
    values = values.at[picks[0]].set(KMAX).at[picks[1]].set(KMAX // 8)
    return values.reshape(N_ROW, N_COL).astype(jnp.int32)


def block_scale(stream_key, shape, shards, least, largest):
    gain = 1.0
    for position, shards_of in shards:
        heights = jax.random.uniform(jax.random.fold_in(jax.random.fold_in(stream_key, 6), position), (shards_of,), jnp.float32, least / len(shards), largest / len(shards))
        gain = gain * jnp.repeat(jnp.exp(heights), shape[position] // shards_of).reshape((-1,) + (1,) * (len(shape) - 1 - position))
    return gain


def gaussian(key, dims, spread, bound, cuts=(), held_as=jnp.bfloat16):
    result = jax.random.normal(key, dims, jnp.float32) * spread
    if len(cuts) > 0:
        result = block_scale(key, dims, cuts, -0.22, 0.18) * result
    return jnp.clip(result, min=-bound, max=bound).astype(held_as)


def setup_inputs(seed: int = 0) -> dict:
    keys = jax.random.split(jax.random.key(seed), 8)
    features = gaussian(keys[0], (NODES, F), 1.0, 6.0, ((0, 128),))
    weight = gaussian(keys[1], (F, FO), F ** -0.5, 0.375, ((1, 2),))
    bias = gaussian(keys[2], (FO,), 0.5, 3.0, ((0, 2),), jnp.float32)
    blocks = gaussian(keys[3], (N_ROW, N_COL, KMAX, BS, BS), (max(1, BS * N_COL * KMAX // (2 * RB))) ** -0.5, 0.09375, ((0, 8), (1, 16)))
    coords = draw_coords(jax.random.fold_in(keys[7], 71), 0)
    counts = draw_counts(jax.random.fold_in(keys[7], 71), 0)
    cotangent = gaussian(keys[6], (NODES, FO), 1.0, 6.0, ((0, 128), (1, 2)))
    return {"features": features, "weight": weight, "bias": bias, "blocks": blocks, "coords": coords, "counts": counts, "cotangent": cotangent}


def spread_ref(block_set, take_index, put_index, active, source, segment_count, transpose):
    block_size = block_set.shape[-1]
    feature_width = source.shape[1]
    pieces = source.reshape(-1, block_size, feature_width)[take_index].astype(jnp.float32)
    einsum_form = 'kji,kjf->kif' if transpose else 'kij,kjf->kif'
    products = jnp.einsum(einsum_form, block_set.astype(jnp.float32), pieces)
    targets = jnp.where(active, put_index, segment_count)
    summed = jax.ops.segment_sum(products, targets, num_segments=segment_count + 1)
    return summed[:segment_count].reshape(segment_count * block_size, feature_width)


def reference(features, weight, bias, blocks, coords, counts, cotangent):
    xw_all = jnp.dot(features, weight, preferred_element_type=jnp.float32).astype(jnp.bfloat16)
    slot_ids = jnp.arange(KMAX, dtype=jnp.int32)

    def forward_tile(index, total):
        row_id = index // N_COL
        col_id = index % N_COL
        block_set = blocks[row_id, col_id]
        place = coords[row_id, col_id]
        active = slot_ids < counts[row_id, col_id]
        source = lax.dynamic_slice_in_dim(xw_all, (col_id * CB * BS).astype(jnp.int32), CB * BS, 0)
        partial_value = spread_ref(block_set, place[:, 1], place[:, 0], active, source, RB, False)
        start = (row_id * RB * BS).astype(jnp.int32)
        current = lax.dynamic_slice_in_dim(total, start, RB * BS, 0)
        return lax.dynamic_update_slice_in_dim(total, current + partial_value, start, 0)

    aggregate = lax.fori_loop(0, N_ROW * N_COL, forward_tile, jnp.zeros((NODES, FO), jnp.float32))
    pre_act = aggregate + bias
    sigmoid_z = jax.nn.sigmoid(pre_act)
    outputs = (pre_act * sigmoid_z).astype(jnp.bfloat16)
    grad_z = (cotangent.astype(jnp.float32) * sigmoid_z * (1.0 + pre_act * (1.0 - sigmoid_z))).astype(jnp.bfloat16)

    def backward_tile(index, total):
        row_id = index // N_COL
        col_id = index % N_COL
        block_set = blocks[row_id, col_id]
        place = coords[row_id, col_id]
        active = slot_ids < counts[row_id, col_id]
        source = lax.dynamic_slice_in_dim(grad_z, (row_id * RB * BS).astype(jnp.int32), RB * BS, 0)
        partial_value = spread_ref(block_set, place[:, 0], place[:, 1], active, source, CB, True)
        start = (col_id * CB * BS).astype(jnp.int32)
        current = lax.dynamic_slice_in_dim(total, start, CB * BS, 0)
        return lax.dynamic_update_slice_in_dim(total, current + partial_value, start, 0)

    grad_xw = lax.fori_loop(0, N_ROW * N_COL, backward_tile, jnp.zeros((NODES, FO), jnp.float32)).astype(jnp.bfloat16)
    grad_in = jnp.einsum('no,fo->nf', grad_xw.astype(jnp.float32), weight.astype(jnp.float32)).astype(jnp.bfloat16)
    grad_w = jnp.einsum('nf,no->fo', features.astype(jnp.float32), grad_xw.astype(jnp.float32))
    grad_b = jnp.sum(grad_z.astype(jnp.float32), axis=0)
    return outputs, grad_in, grad_w, grad_b
```

```python
import functools

import jax
import jax.numpy as jnp
from jax import lax
from jax.experimental import pallas as pl
from jax.experimental.pallas import tpu as pltpu
from jax.sharding import PartitionSpec as P

BF = jnp.bfloat16
F32 = jnp.float32
MESH = pl.DeviceIdType.MESH
VMEM = pl.BlockSpec(memory_space=pltpu.VMEM)
SMEM = pl.BlockSpec(memory_space=pltpu.SMEM)
ANY = pl.BlockSpec(memory_space=pl.ANY)
LIMIT = 56 * 1024 * 1024
UNROLL = 8


class Net:
    def __init__(self, send_sems, recv_sems):
        self.send_sems, self.recv_sems, self.copies = send_sems, recv_sems, []

    def send(self, src, dst, device):
        index = len(self.copies)
        copy = pltpu.make_async_remote_copy(
            src_ref=src,
            dst_ref=dst,
            send_sem=self.send_sems.at[index],
            recv_sem=self.recv_sems.at[index],
            device_id=device,
            device_id_type=MESH,
        )
        copy.start()
        self.copies.append(copy)
        return copy

    def drain(self):
        for copy in self.copies:
            copy.wait_send()


def greet(devices):
    barrier = pltpu.get_barrier_semaphore()
    for device in devices:
        pl.semaphore_signal(barrier, inc=1, device_id=device, device_id_type=MESH)
    return lambda: pl.semaphore_wait(barrier, len(devices))


def interleave(streams):
    streams = list(streams)
    while streams:
        alive = []
        for stream in streams:
            try:
                next(stream)
                alive.append(stream)
            except StopIteration:
                pass
        streams = alive


def wrap(index, size):
    return lax.rem(index + 2 * size, size)


def gather_xw(feat_ref, w_ref, xw_ref, wfull_ref, send_sems, recv_sems):
    row = lax.axis_index("row")
    y, core = row // 2, lax.rem(row, 2)
    f = lax.axis_index("feat")
    sib = {"row": y * 2 + 1 - core}
    up = {"row": wrap(y + 1, 4) * 2 + core}
    down = {"row": wrap(y - 1, 4) * 2 + core}
    other = {"feat": 1 - f}
    wait = greet([sib, up, down, other])
    xw_ref[row] = jnp.dot(feat_ref[...], w_ref[...], preferred_element_type=F32).astype(BF)
    wfull_ref[f] = w_ref[...]
    wait()
    net = Net(send_sems, recv_sems)
    half = [pl.ds(0, 192), pl.ds(192, 192)]

    def move(slot, part, device):
        ref = xw_ref.at[slot, half[part]]
        return net.send(ref, ref, device)

    u = [move(row, 0, up), None]
    d = [None, move(row, 1, down)]
    u[1] = move(row, 1, up)
    d[0] = move(row, 0, down)
    s = [move(row, 0, sib), move(row, 1, sib)]
    wcopy = net.send(w_ref, wfull_ref.at[f], other)
    lower = wrap(y - 1, 4) * 2 + core
    upper = wrap(y + 1, 4) * 2 + core
    far = wrap(y + 2, 4) * 2 + core
    u[0].wait_recv()
    u2 = move(lower, 0, up)
    s.append(move(lower, 0, sib))
    d[1].wait_recv()
    d2 = move(upper, 1, down)
    s.append(move(upper, 1, sib))
    u[1].wait_recv()
    s.append(move(lower, 1, sib))
    d[0].wait_recv()
    s.append(move(upper, 0, sib))
    u2.wait_recv()
    s.append(move(far, 0, sib))
    d2.wait_recv()
    s.append(move(far, 1, sib))
    wcopy.wait_recv()
    for copy in s:
        copy.wait_recv()
    net.drain()


def spmm(count_ref, coord_ref, src_ref, blocks_ref, out_ref, blk, acc, sems, *, transpose):
    slots = blk.shape[0]
    parts = sems.shape[0]
    size = slots // parts
    targets = out_ref.shape[0]

    def fetch(part):
        span = pl.ds(part * size, size)
        return pltpu.make_async_copy(blocks_ref.at[span], blk.at[span], sems.at[part])

    for part in range(parts):
        fetch(part).start()
    acc[...] = jnp.zeros_like(acc)
    count = count_ref[0]

    def chunk(part, carry):
        fetch(part).wait()
        base = part * size
        groups = jnp.clip((count - base + UNROLL - 1) // UNROLL, 0, size // UNROLL)

        def group(g, carry):
            start = base + g * UNROLL
            for u in range(UNROLL):
                k = start + u
                i, j = coord_ref[0, k], coord_ref[1, k]
                take, put = (i, j) if transpose else (j, i)
                put = jnp.where(k < count, put, targets)
                if transpose:
                    prod = jnp.dot(src_ref[take], blk[k], preferred_element_type=F32)
                else:
                    prod = jnp.dot(blk[k], src_ref[take], preferred_element_type=F32)
                acc[put] += prod
            return carry

        return lax.fori_loop(0, groups, group, carry)

    lax.fori_loop(0, parts, chunk, 0)

    def cast(t, carry):
        out_ref[t] = acc[t].astype(BF)
        return carry

    lax.fori_loop(0, targets, cast, 0)


def call_spmm(count, coord, src, blocks, targets, transpose):
    parts = 8
    return pl.pallas_call(
        functools.partial(spmm, transpose=transpose),
        out_shape=jax.ShapeDtypeStruct((targets, 128, 128), BF),
        in_specs=[SMEM, SMEM, VMEM, ANY],
        out_specs=VMEM,
        scratch_shapes=[
            pltpu.VMEM(blocks.shape, BF),
            pltpu.VMEM((targets + 1, 128, 128), F32),
            pltpu.SemaphoreType.DMA((parts,)),
        ],
        compiler_params=pltpu.CompilerParams(vmem_limit_bytes=LIMIT),
        name="spmm_bwd" if transpose else "spmm_fwd",
    )(count, coord, src, blocks)


def middle(p_ref, bias_ref, cot_ref, out_ref, g_ref, bsum_ref, rp, rm, sp, sm, xr, xs, send_sems, recv_sems):
    col = lax.axis_index("col")
    z, x = col // 2, lax.rem(col, 2)
    nbr = {"col": z * 2 + 1 - x}
    up = {"col": wrap(z + 1, 8) * 2 + x}
    down = {"col": wrap(z - 1, 8) * 2 + x}
    greet([nbr, up, down])()
    net = Net(send_sems, recv_sems)
    A, B, ALL = pl.ds(0, 64), pl.ds(64, 64), pl.ds(0, 128)

    def part(c, b, rows=ALL):
        return p_ref[c, b, rows].astype(F32)

    def ring_z(b, width, own):
        last = None
        for t in range(4):
            du, dd = wrap(z + 4 - t, 8), wrap(z - 4 + t, 8)
            if t:
                yield
                last[0].wait_recv()
                last[1].wait_recv()
            for i in range(width):
                if t == 0:
                    sp[b, t, i, A] = own(du, i, A, t, 0).astype(BF)
                    sm[b, t, i, B] = own(dd, i, B, t, 1).astype(BF)
                elif t == 1:
                    sp[b, t, i, A] = (own(du, i, A, t, 0) + rp[b, 0, i, A].astype(F32)).astype(BF)
                    sp[b, t, i, B] = own(du, i, B, t, 0).astype(BF)
                    sm[b, t, i, A] = own(dd, i, A, t, 1).astype(BF)
                    sm[b, t, i, B] = (own(dd, i, B, t, 1) + rm[b, 0, i, B].astype(F32)).astype(BF)
                else:
                    sp[b, t, i] = (own(du, i, ALL, t, 0) + rp[b, t - 1, i].astype(F32)).astype(BF)
                    sm[b, t, i] = (own(dd, i, ALL, t, 1) + rm[b, t - 1, i].astype(F32)).astype(BF)
            span = pl.ds(0, width)
            rows = (A, B) if t == 0 else (ALL, ALL)
            last = (
                net.send(sp.at[b, t, span, rows[0]], rp.at[b, t, span, rows[0]], up),
                net.send(sm.at[b, t, span, rows[1]], rm.at[b, t, span, rows[1]], down),
            )
        yield
        last[0].wait_recv()
        last[1].wait_recv()

    def reduce_z_first(b):
        yield from ring_z(b, 2, lambda d, i, rows, t, side: part(d * 2 + i, b, rows))

        def full(i):
            return part(z * 2 + i, b) + rp[b, 3, i].astype(F32) + rm[b, 3, i].astype(F32)

        xs[b] = full(1 - x).astype(BF)
        copy = net.send(xs.at[b], xr.at[b, 0], nbr)
        mine = full(x)
        yield
        copy.wait_recv()
        return mine + xr[b, 0].astype(F32)

    def reduce_x_first(b):
        copies = {}
        for k in (4, 3, -3, 2, -2, 1, -1, 0):
            d = wrap(z + k, 8)
            copies[k] = net.send(p_ref.at[d * 2 + 1 - x, b], xr.at[b, k % 8], nbr)
        waited = set()

        def own(d, i, rows, t, side):
            k = 0 if t is None else 4 - t if side == 0 or t == 0 else t - 4
            if k not in waited:
                copies[k].wait_recv()
                waited.add(k)
            return part(d * 2 + x, b, rows) + xr[b, k % 8, rows].astype(F32)

        yield
        yield from ring_z(b, 1, own)
        return own(z, 0, ALL, None, 0) + rp[b, 3, 0].astype(F32) + rm[b, 3, 0].astype(F32)

    def activate(b, total):
        rows = pl.ds(b * 128, 128)
        pre = total + bias_ref[...]
        s = 1.0 / (1.0 + jnp.exp(-pre))
        out_ref[rows] = (pre * s).astype(BF)
        gz = (cot_ref[rows].astype(F32) * s * (1.0 + pre * (1.0 - s))).astype(BF).astype(F32)
        bsum_ref[b] = jnp.sum(gz.reshape(16, 8, 128), axis=0)
        g_ref[col, b] = gz.T.astype(BF)

    def gather_z_first(b):
        def move(slot, device, rows=ALL):
            ref = g_ref.at[slot, b, rows]
            return net.send(ref, ref, device)

        to_x = []
        ups, downs = move(col, up), move(col, down)
        to_x.append(move(col, nbr))
        for t in range(1, 5):
            yield
            src = wrap(z - t, 8) * 2 + x
            ups.wait_recv()
            if t < 4:
                ups = move(src, up, ALL if t < 3 else A)
            to_x.append(move(src, nbr, ALL if t < 4 else A))
            src = wrap(z + t, 8) * 2 + x
            downs.wait_recv()
            if t < 4:
                downs = move(src, down, ALL if t < 3 else B)
            to_x.append(move(src, nbr, ALL if t < 4 else B))
        yield
        for copy in to_x:
            copy.wait_recv()

    def gather_x_first(b):
        def move(zz, device, rows=ALL):
            ref = g_ref.at[pl.ds(zz * 2, 2), b, rows]
            return net.send(ref, ref, device)

        ref = g_ref.at[col, b]
        first = net.send(ref, ref, nbr)
        yield
        first.wait_recv()
        ups, downs = move(z, up), move(z, down)
        for t in range(1, 5):
            yield
            ups.wait_recv()
            if t < 4:
                ups = move(wrap(z - t, 8), up, ALL if t < 3 else A)
            downs.wait_recv()
            if t < 4:
                downs = move(wrap(z + t, 8), down, ALL if t < 3 else B)

    def stream(b, reduce, gather):
        total = yield from reduce(b)
        activate(b, total)
        yield from gather(b)

    interleave([
        stream(0, reduce_z_first, gather_x_first),
        stream(1, reduce_x_first, gather_z_first),
        stream(2, reduce_x_first, gather_x_first),
    ])
    net.drain()


def finish(
    p_ref, feat_ref, wfull_ref, bsum_ref, gin_ref, gw_ref, gb_ref,
    cr, rp, rm, sp, sm, g, h, gin, part, w1, w2, w3, wx, xin, send_sems, recv_sems,
):
    row = lax.axis_index("row")
    y, core = row // 2, lax.rem(row, 2)
    col = lax.axis_index("col")
    z, x = col // 2, lax.rem(col, 2)
    f = lax.axis_index("feat")
    sib = {"row": y * 2 + 1 - core}
    up = {"row": wrap(y + 1, 4) * 2 + core}
    down = {"row": wrap(y - 1, 4) * 2 + core}
    other = {"feat": 1 - f}
    rows_of = [{"row": wrap(row + k, 8)} for k in range(1, 8)]
    nbr = {"col": z * 2 + 1 - x}
    zs_of = [{"col": wrap(z + k, 8) * 2 + x} for k in range(1, 8)]
    greet(rows_of + zs_of + [nbr, other])()
    net = Net(send_sems, recv_sems)
    A, B, ALL = pl.ds(0, 64), pl.ds(64, 64), pl.ds(0, 128)

    def reduce(b):
        copies = {}
        for k in (2, 1, -1, 0):
            d = wrap(y + k, 4)
            copies[k] = net.send(p_ref.at[d * 2 + 1 - core, b], cr.at[b, k % 4], sib)
        yield

        def own(k, rows):
            slot = wrap(y + k, 4) * 2 + core
            return p_ref[slot, b, rows].astype(F32) + cr[b, k % 4, rows].astype(F32)

        copies[2].wait_recv()
        sp[b, 0, A] = own(2, A).astype(BF)
        sm[b, 0, B] = own(2, B).astype(BF)
        u = net.send(sp.at[b, 0, A], rp.at[b, 0, A], up)
        d = net.send(sm.at[b, 0, B], rm.at[b, 0, B], down)
        yield
        copies[1].wait_recv()
        u.wait_recv()
        sp[b, 1, A] = (own(1, A) + rp[b, 0, A].astype(F32)).astype(BF)
        sp[b, 1, B] = own(1, B).astype(BF)
        u = net.send(sp.at[b, 1], rp.at[b, 1], up)
        copies[-1].wait_recv()
        d.wait_recv()
        sm[b, 1, A] = own(-1, A).astype(BF)
        sm[b, 1, B] = (own(-1, B) + rm[b, 0, B].astype(F32)).astype(BF)
        d = net.send(sm.at[b, 1], rm.at[b, 1], down)
        yield
        copies[0].wait_recv()
        u.wait_recv()
        d.wait_recv()
        g[b] = (own(0, ALL) + rp[b, 1].astype(F32) + rm[b, 1].astype(F32)).astype(BF)

    interleave([reduce(b) for b in range(3)])

    halves = net.send(g.at[pl.ds(1 - f, 2)], h, other)
    gwt = jnp.zeros((128, 256), F32)
    for b in range(3):
        gwt += jnp.dot(g[b], feat_ref[pl.ds(b * 128, 128)], preferred_element_type=F32)
    for r in range(8):
        part[r, 0:16] = gwt[r * 16:(r + 1) * 16]
        part[r, 16:24, 0:128] = bsum_ref[0] + bsum_ref[1] + bsum_ref[2]
        part[r, 16:24, 128:256] = jnp.zeros((8, 128), F32)
    copies = []
    for k in range(1, 8):
        copies.append(net.send(part.at[wrap(row + k, 8)], w1.at[row], rows_of[k - 1]))
    w1[row] = part[row]

    halves.wait_recv()
    for n in range(2):
        block = jnp.dot(wfull_ref[f], g[f + n], preferred_element_type=F32)
        block += jnp.dot(wfull_ref[1 - f], h[n], preferred_element_type=F32)
        gin[pl.ds(n * 128, 128)] = block.T.astype(BF)
    gin_ref[...] = gin[pl.ds(pl.multiple_of(f * 64, 64), 192)]

    for copy in copies:
        copy.wait_recv()
    total = w1[0]
    for r in range(1, 8):
        total += w1[r]
    wx[...] = total
    copy = net.send(wx, xin, nbr)
    copy.wait_recv()
    w2[z] = wx[...] + xin[...]
    copies = [net.send(w2.at[z], w2.at[z], zs_of[k - 1]) for k in range(1, 8)]
    for copy in copies:
        copy.wait_recv()
    total = w2[0]
    for r in range(1, 8):
        total += w2[r]
    w3[row] = total[0:16]
    gb_ref[...] = jnp.sum(total[16:24, 0:128], axis=0, keepdims=True)
    copies = [net.send(w3.at[row], w3.at[row], rows_of[k - 1]) for k in range(1, 8)]
    for copy in copies:
        copy.wait_recv()
    gw_ref[...] = w3[...].reshape(128, 256).T
    net.drain()


def remote_call(kernel, name, collective_id, out_shape, operands, scratch, copies):
    return pl.pallas_call(
        kernel,
        out_shape=out_shape,
        in_specs=[VMEM] * len(operands),
        out_specs=[VMEM] * len(out_shape),
        scratch_shapes=scratch
        + [pltpu.SemaphoreType.DMA((copies,)), pltpu.SemaphoreType.DMA((copies,))],
        compiler_params=pltpu.CompilerParams(
            collective_id=collective_id, has_side_effects=True, vmem_limit_bytes=LIMIT
        ),
        name=name,
    )(*operands)


def body(features, weight, bias, blocks, coords, counts, cotangent):
    blocks = blocks[0, 0]
    coord = coords[0, 0].T
    count = counts[0]
    shape = jax.ShapeDtypeStruct
    xw, wfull = remote_call(
        gather_xw, "gather_xw", 1,
        [shape((8, 384, 128), BF), shape((2, 256, 128), BF)],
        [features, weight], [], 16,
    )
    partial = call_spmm(count, coord, xw.reshape(24, 128, 128), blocks, 48, False)
    tile = (128, 128)
    outputs, g, bsum = remote_call(
        middle, "middle", 2,
        [shape((384, 128), BF), shape((16, 3) + tile, BF), shape((3, 8, 128), F32)],
        [partial.reshape((16, 3) + tile), bias.reshape(1, 128), cotangent],
        [
            pltpu.VMEM((3, 4, 2) + tile, BF),
            pltpu.VMEM((3, 4, 2) + tile, BF),
            pltpu.VMEM((3, 4, 2) + tile, BF),
            pltpu.VMEM((3, 4, 2) + tile, BF),
            pltpu.VMEM((3, 8) + tile, BF),
            pltpu.VMEM((3,) + tile, BF),
        ],
        80,
    )
    grads = call_spmm(count, coord, g.reshape((48,) + tile), blocks, 24, True)
    grad_in, grad_w, grad_b = remote_call(
        finish, "finish", 3,
        [shape((192, 256), BF), shape((256, 128), F32), shape((1, 128), F32)],
        [grads.reshape((8, 3) + tile), features, wfull, bsum],
        [
            pltpu.VMEM((3, 4) + tile, BF),
            pltpu.VMEM((3, 2) + tile, BF),
            pltpu.VMEM((3, 2) + tile, BF),
            pltpu.VMEM((3, 2) + tile, BF),
            pltpu.VMEM((3, 2) + tile, BF),
            pltpu.VMEM((3,) + tile, BF),
            pltpu.VMEM((2,) + tile, BF),
            pltpu.VMEM((256, 256), BF),
            pltpu.VMEM((8, 24, 256), F32),
            pltpu.VMEM((8, 24, 256), F32),
            pltpu.VMEM((8, 24, 256), F32),
            pltpu.VMEM((8, 16, 256), F32),
            pltpu.VMEM((24, 256), F32),
            pltpu.VMEM((24, 256), F32),
        ],
        50,
    )
    return outputs, grad_in, grad_w, grad_b.reshape(128)


def solution(mesh):
    in_specs = (
        P(("col", "row"), None),
        P(None, "feat"),
        P("feat"),
        P("row", "col", None, None, None),
        P("row", "col", None, None),
        P("row", "col"),
        P(("row", "col"), "feat"),
    )
    out_specs = (
        P(("row", "col"), "feat"),
        P(("col", "row", "feat"), None),
        P(None, "feat"),
        P("feat"),
    )
    return jax.shard_map(body, mesh=mesh, in_specs=in_specs, out_specs=out_specs, check_vma=False)
```

```python
import functools

import jax
import jax.numpy as jnp
from jax import lax
from jax.experimental import pallas as pl
from jax.experimental.pallas import tpu as pltpu
from jax.sharding import PartitionSpec as P

BF = jnp.bfloat16
F32 = jnp.float32
MESH = pl.DeviceIdType.MESH
VMEM = pl.BlockSpec(memory_space=pltpu.VMEM)
SMEM = pl.BlockSpec(memory_space=pltpu.SMEM)
ANY = pl.BlockSpec(memory_space=pl.ANY)
LIMIT = 62 * 1024 * 1024


class Net:
    def __init__(self, send_sems, recv_sems):
        self.send_sems, self.recv_sems, self.copies = send_sems, recv_sems, []

    def send(self, src, dst, device):
        index = len(self.copies)
        copy = pltpu.make_async_remote_copy(
            src_ref=src,
            dst_ref=dst,
            send_sem=self.send_sems.at[index],
            recv_sem=self.recv_sems.at[index],
            device_id=device,
            device_id_type=MESH,
        )
        copy.start()
        self.copies.append(copy)
        return copy

    def drain(self):
        for copy in self.copies:
            copy.wait_send()


def greet(devices):
    barrier = pltpu.get_barrier_semaphore()
    for device in devices:
        pl.semaphore_signal(barrier, inc=1, device_id=device, device_id_type=MESH)
    return lambda: pl.semaphore_wait(barrier, len(devices))


def interleave(streams):
    streams = list(streams)
    while streams:
        alive = []
        for stream in streams:
            try:
                next(stream)
                alive.append(stream)
            except StopIteration:
                pass
        streams = alive


def wrap(index, size):
    return lax.rem(index + 2 * size, size)


def order_slots(coord, count, key, targets, lists, work):
    size, half = 256, 128
    work[0:2, :] = jnp.full((2, size), 63.0, F32)
    work[0:2, 0:192] = coord[...].astype(F32)
    one, zero = jnp.float32(1.0), jnp.float32(0.0)
    lane = lax.broadcasted_iota(jnp.int32, (size, size), 1)
    sub = lax.broadcasted_iota(jnp.int32, (size, size), 0)
    keys = jnp.where(lane[0:1] < count, work[key:key + 1, :], 63.0)
    takes = work[1 - key:2 - key, :]
    key_of = jnp.broadcast_to(keys, (half, size)).T
    wide = jnp.concatenate([key_of, key_of], axis=1)
    same = jnp.where(wide == keys, one, zero)
    rank_row = jnp.sum(jnp.where(sub < lane, same, zero), axis=0, keepdims=True)
    rank = jnp.dot(
        jnp.where(lane < sub, same, zero).astype(BF), jnp.ones((size, half), BF), preferred_element_type=F32
    )
    member = jnp.where(key_of == lane[:, :half].astype(F32), one, zero)
    number = jnp.sum(member, axis=0, keepdims=True)
    number = jnp.where(lane[0:1, :half] < targets, number, zero)
    steps = jnp.floor((number + 1.0) * 0.5)
    lower = jnp.where(sub[:half, :half] < lane[:half, :half], one, zero).astype(BF)
    start = jnp.dot(jnp.broadcast_to(steps, (half, half)).astype(BF), lower, preferred_element_type=F32)
    start_of = lax.dot_general(
        member.astype(BF), start.astype(BF), (((1,), (1,)), ((), ())), preferred_element_type=F32
    )
    place = jnp.where(key_of > 62.0, -1.0, 2.0 * start_of + rank)
    lane_f = lane.astype(F32)
    hit = jnp.where(jnp.concatenate([place, place], axis=1) == lane_f, one, zero).astype(BF)
    kind = sub[0:16]
    opens = jnp.where(rank_row == 0.0, one, zero)
    values = jnp.where(kind == 0, lane_f[0:16] - 192.0, jnp.where(kind == 1, takes, jnp.where(kind == 2, opens, zero)))
    found = jnp.dot(values.astype(BF), hit, preferred_element_type=F32).astype(jnp.int32)
    lists[0:1, :] = jnp.clip(found[0:1] + 192, 0, 192)
    lists[1:2, :] = jnp.clip(found[1:2], 0, 71 - targets)
    lists[2:3, :] = jnp.clip(found[2:3], 0, 1)
    lists[3:4, 0:half] = jnp.clip((start[0:1] + steps - 1.0).astype(jnp.int32), 0, 95 + targets // 2)
    lists[4:5, 0:half] = jnp.where(number > 0.0, 1, 0)


def products(table, blk, src, run_of, steps, unroll, transpose):
    def group(i, run):
        for u in range(unroll):
            q = i * unroll + u
            s0, s1 = table[0, 2 * q], table[0, 2 * q + 1]
            t0, t1 = table[1, 2 * q], table[1, 2 * q + 1]
            if transpose:
                lhs = jnp.concatenate([src[t0], src[t1]], axis=1)
                rhs = jnp.concatenate([blk[s0], blk[s1]], axis=0)
            else:
                lhs = jnp.concatenate([blk[s0], blk[s1]], axis=1)
                rhs = jnp.concatenate([src[t0], src[t1]], axis=0)
            prod = jnp.dot(lhs, rhs, preferred_element_type=F32)
            run = jnp.where(table[2, 2 * q] == 1, 0.0, run) + prod
            run_of[q] = run
        return run

    lax.fori_loop(0, steps // unroll, group, jnp.zeros((128, 128), F32))


def layer(
    feat_ref, w_ref, bias_ref, coord_ref, count_ref, cot_ref, blocks_ref,
    out_ref, gin_ref, gw_ref, gb_ref,
    xw, fall, wfull, blk, run_of, p, g, rp, rm, sp, sm, dp, dm, xr,
    p5, cr, rp5, sp5, g5, h, gin, part5, w1, w2, w3, bsend, brecv,
    coord, bias, cot, work, lists, table, send_sems, recv_sems, local_sems,
):
    row = lax.axis_index("row")
    y, core = row // 2, lax.rem(row, 2)
    col = lax.axis_index("col")
    z, x = col // 2, lax.rem(col, 2)
    f = lax.axis_index("feat")
    sib = {"row": y * 2 + 1 - core}
    yup = {"row": wrap(y + 1, 4) * 2 + core}
    ydown = {"row": wrap(y - 1, 4) * 2 + core}
    yfar = {"row": wrap(y + 2, 4) * 2 + core}
    other = {"feat": 1 - f}
    nbr = {"col": z * 2 + 1 - x}
    up = {"col": wrap(z + 1, 8) * 2 + x}
    down = {"col": wrap(z - 1, 8) * 2 + x}
    up_x = {"col": wrap(z + 1, 8) * 2 + 1 - x}
    down_x = {"col": wrap(z - 1, 8) * 2 + 1 - x}
    rows_of = [{"row": wrap(row + k, 8)} for k in range(1, 8)]
    cols_of = [{"col": wrap(col + k, 16)} for k in range(1, 16)]
    wait = greet(rows_of + cols_of + [other])
    net = Net(send_sems, recv_sems)
    A, B, ALL, THREE = pl.ds(0, 64), pl.ds(64, 64), pl.ds(0, 128), pl.ds(0, 3)

    fetches = []

    def fetch(src, dst):
        copy = pltpu.make_async_copy(src, dst, local_sems.at[len(fetches)])
        copy.start()
        fetches.append(copy)

    fetch(feat_ref, fall.at[row])
    fetch(w_ref, wfull.at[f])
    fetch(coord_ref, coord)
    fetch(bias_ref, bias)
    fetch(cot_ref, cot)
    for n in range(4):
        span = pl.ds(n * 48, 48)
        fetch(blocks_ref.at[span], blk.at[span])
    fetches[0].wait()
    fetches[1].wait()
    own = jnp.dot(fall[row].reshape(384, 256), wfull[f], preferred_element_type=F32).astype(BF)
    xw[row] = own.reshape(3, 128, 128)
    blk[192] = jnp.zeros((128, 128), BF)
    wait()

    def gather_row(buf):
        def move(slot, device, rows=ALL):
            ref = buf.at[slot, THREE, rows]
            return net.send(ref, ref, device)

        lower = wrap(y - 1, 4) * 2 + core
        upper = wrap(y + 1, 4) * 2 + core
        far = wrap(y + 2, 4) * 2 + core
        u0, d1 = move(row, yup, A), move(row, ydown, B)
        u1, d0 = move(row, yup, B), move(row, ydown, A)
        s = [move(row, sib)]
        yield
        u0.wait_recv()
        u2 = move(lower, yup, A)
        d1.wait_recv()
        d2 = move(upper, ydown, B)
        yield
        u1.wait_recv()
        s.append(move(lower, sib))
        d0.wait_recv()
        s.append(move(upper, sib))
        yield
        u2.wait_recv()
        d2.wait_recv()
        s.append(move(far, sib))
        yield
        for copy in s:
            copy.wait_recv()

    def order(n, key, targets):
        order_slots(coord, count_ref[0], key, targets, lists.at[n], work)
        fetch(lists.at[n], table.at[n])
        yield

    fetches[2].wait()
    interleave([gather_row(xw), order(0, 0, 48)])
    features_to_all = gather_row(fall)
    next(features_to_all)
    wcopy = net.send(wfull.at[f], wfull.at[f], other)
    for copy in fetches[3:]:
        copy.wait()
    fetches.clear()
    products(table.at[0], blk, xw.reshape(24, 128, 128), run_of, 120, 24, False)

    def summed(n, t):
        return jnp.where(table[n, 4, t] == 1, run_of[table[n, 3, t]], 0.0)

    starts = {}

    def place(k, side):
        shard = wrap(z + k, 8) * 2 + side
        for b in range(3):
            p[shard, b] = summed(0, shard * 3 + b).astype(BF)
        return shard

    shard, cross = place(4, x), place(4, 1 - x)
    for b in range(3):
        starts["u", b] = net.send(p.at[shard, b, A], rp.at[0, b, A], up)
        starts["d", b] = net.send(p.at[shard, b, B], rm.at[0, b, B], down)
        starts["u4", b] = net.send(p.at[cross, b, A], dp.at[0, b, A], up_x)
        starts["d4", b] = net.send(p.at[cross, b, B], dm.at[0, b, B], down_x)
    for name, k, landing, device in (("u3", 3, dp, up_x), ("d3", -3, dm, down_x)):
        shard = place(k, 1 - x)
        for b in range(3):
            starts[name, b] = net.send(p.at[shard, b], landing.at[1, b], device)
    for k in (2, -2, 1, -1, 0):
        shard = place(k, 1 - x)
        for b in range(3):
            starts[k, b] = net.send(p.at[shard, b], xr.at[k % 8, b], nbr)

    def own(k, b):
        return summed(0, (wrap(z + k, 8) * 2 + x) * 3 + b)

    def wide(ref):
        return ref.astype(F32)

    def reduce_col(b):
        u, d = starts["u", b], starts["d", b]
        u.wait_recv()
        starts["u4", b].wait_recv()
        value = own(3, b)
        sp[1, b, A] = (value[:64] + wide(rp[0, b, A]) + wide(dp[0, b, A])).astype(BF)
        sp[1, b, B] = value[64:].astype(BF)
        u = net.send(sp.at[1, b], rp.at[1, b], up)
        d.wait_recv()
        starts["d4", b].wait_recv()
        value = own(-3, b)
        sm[1, b, A] = value[:64].astype(BF)
        sm[1, b, B] = (value[64:] + wide(rm[0, b, B]) + wide(dm[0, b, B])).astype(BF)
        d = net.send(sm.at[1, b], rm.at[1, b], down)
        yield
        for t in (2, 3):
            k = 4 - t
            u.wait_recv()
            starts[k, b].wait_recv()
            value = own(k, b) + wide(xr[k, b]) + wide(rp[t - 1, b])
            if t == 2:
                starts["u3", b].wait_recv()
                value += wide(dp[1, b])
            sp[t, b] = value.astype(BF)
            u = net.send(sp.at[t, b], rp.at[t, b], up)
            d.wait_recv()
            starts[-k, b].wait_recv()
            value = own(-k, b) + wide(xr[8 - k, b]) + wide(rm[t - 1, b])
            if t == 2:
                starts["d3", b].wait_recv()
                value += wide(dm[1, b])
            sm[t, b] = value.astype(BF)
            d = net.send(sm.at[t, b], rm.at[t, b], down)
            yield
        starts[0, b].wait_recv()
        value = own(0, b) + wide(xr[0, b])
        u.wait_recv()
        d.wait_recv()
        return value + wide(rp[3, b]) + wide(rm[3, b])

    def activate(b, total):
        rows = pl.ds(b * 128, 128)
        pre = total + bias[...]
        s = 1.0 / (1.0 + jnp.exp(-pre))
        out_ref[rows] = (pre * s).astype(BF)
        gz = cot[rows].astype(F32) * s * (1.0 + pre * (1.0 - s))
        g[col, b] = gz.T.astype(BF)

    def gather_col(b):
        def move(slot, device, rows=ALL):
            ref = g.at[slot, b, rows]
            return net.send(ref, ref, device)

        rest = []
        last = {1: move(col, up), -1: move(col, down)}
        rest.append(move(col, nbr))
        for hop in range(1, 5):
            yield
            for sign, device, cross, rows in ((1, up, up_x, A), (-1, down, down_x, B)):
                slot = wrap(z - sign * hop, 8) * 2 + x
                last[sign].wait_recv()
                if hop < 4:
                    part = ALL if hop < 3 else rows
                    last[sign] = move(slot, device, part)
                    if hop < 3:
                        if hop == 2:
                            rest.append(move(slot, cross))
                        rest.append(move(slot, nbr))
                    else:
                        rest.append(move(slot, cross, rows))
        yield
        for copy in rest:
            copy.wait_recv()

    def stream(b):
        total = yield from reduce_col(b)
        activate(b, total)
        yield from gather_col(b)

    interleave([stream(0), stream(1), stream(2), order(1, 1, 24), features_to_all])
    fetches[0].wait()

    products(table.at[1], blk, g.reshape(48, 128, 128), run_of, 108, 27, True)

    to_core = {}
    for k in (2, 1, -1, 0):
        shard = wrap(y + k, 4) * 2 + 1 - core
        for b in range(3):
            p5[shard, b] = summed(1, shard * 3 + b).astype(BF)
        to_core[k] = net.send(p5.at[shard], cr.at[k % 4], sib)
    for k in (2, 1, -1, 0):
        shard = wrap(y + k, 4) * 2 + core
        for b in range(3):
            p5[shard, b] = summed(1, shard * 3 + b).astype(BF)

    def mine(k, b, rows):
        slot = wrap(y + k, 4) * 2 + core
        return p5[slot, b, rows].astype(F32) + cr[k % 4, b, rows].astype(F32)

    def input_gradient():
        far = {}
        for b in (1, 0, 2):
            for k, device in ((2, yfar), (1, yup), (-1, ydown)):
                if b == 1:
                    to_core[k].wait_recv()
                sp5[k % 4, b] = mine(k, b, ALL).astype(BF)
                far[k, b] = net.send(sp5.at[k % 4, b], rp5.at[k % 4, b], device)
        yield
        to_core[0].wait_recv()
        halves = []
        for b in (1, 0, 2):
            total = mine(0, b, ALL)
            for k in (1, -1, 2):
                far[k, b].wait_recv()
                total += rp5[k % 4, b].astype(F32)
            g5[b] = total.astype(BF)
            if b == 1:
                halves.append(net.send(g5.at[1], h.at[f], other))
        halves.append(net.send(g5.at[2 - 2 * f], h.at[1 - f], other))
        yield
        wcopy.wait_recv()
        for copy in halves:
            copy.wait_recv()
        for n in range(2):
            block = jnp.dot(wfull[f], g5[f + n], preferred_element_type=F32)
            block += jnp.dot(wfull[1 - f], h[n], preferred_element_type=F32)
            gin[pl.ds(n * 128, 128)] = block.T.astype(BF)
        gin_ref[...] = gin[pl.ds(pl.multiple_of(f * 64, 64), 192)]

    def weight_gradient():
        gwt = jnp.zeros((128, 256), F32)
        for j in range(0, 24, 2):
            a, b = (j // 3, j % 3), ((j + 1) // 3, (j + 1) % 3)
            lhs = jnp.concatenate([p5[a], p5[b]], axis=1)
            rhs = jnp.concatenate([fall[a], fall[b]], axis=0)
            gwt += jnp.dot(lhs, rhs, preferred_element_type=F32)
        for r in range(8):
            part5[r] = gwt[r * 16:(r + 1) * 16]
        copies = []
        for k in range(1, 8):
            copies.append(net.send(part5.at[wrap(row + k, 8)], w1.at[row], rows_of[k - 1]))
        w1[row] = part5[row]
        yield

        def add(t, total):
            return total + g[t // 3, lax.rem(t, 3)].astype(F32)

        nodes = lax.fori_loop(0, 48, add, jnp.zeros((128, 128), F32), unroll=4)
        bsend[...] = jnp.broadcast_to(jnp.sum(nodes.T, axis=0, keepdims=True), (8, 128))
        for copy in copies:
            copy.wait_recv()
        total = w1[0]
        for r in range(1, 8):
            total += w1[r]
        w2[col] = total.astype(BF)
        copies = [net.send(w2.at[col], w2.at[col], cols_of[k - 1]) for k in range(1, 16)]
        biases = [net.send(bsend, brecv.at[row], rows_of[k - 1]) for k in range(1, 8)]
        brecv[row] = bsend[...]
        yield
        for copy in copies:
            copy.wait_recv()
        total = w2[0].astype(F32)
        for c in range(1, 16):
            total += w2[c].astype(F32)
        w3[row] = total
        copies = [net.send(w3.at[row], w3.at[row], rows_of[k - 1]) for k in range(1, 8)]
        for copy in biases:
            copy.wait_recv()
        gb_ref[...] = jnp.sum(brecv[...], axis=0)[0:1]
        yield
        for copy in copies:
            copy.wait_recv()
        gw_ref[...] = w3[...].reshape(128, 256).T

    interleave([weight_gradient(), input_gradient()])
    net.drain()


def emit(*refs):
    for n in range(4):
        refs[4 + n][...] = refs[n][...]


def body(features, weight, bias, blocks, coords, counts, cotangent):
    shape = jax.ShapeDtypeStruct
    tile = (128, 128)

    def vmem(*dims, dtype=BF):
        return pltpu.VMEM(dims, dtype)

    copies = 200
    shapes = [
        shape((384, 128), BF), shape((192, 256), BF), shape((256, 128), F32), shape((1, 128), F32),
    ]
    results = pl.pallas_call(
        layer,
        out_shape=shapes,
        in_specs=[ANY, ANY, ANY, ANY, SMEM, ANY, ANY],
        out_specs=[VMEM] * 4,
        scratch_shapes=[
            vmem(8, 3, *tile), vmem(8, 3, 128, 256), vmem(2, 256, 128), vmem(193, *tile),
            vmem(120, *tile, dtype=F32), vmem(16, 3, *tile), vmem(16, 3, *tile),
            vmem(4, 3, *tile), vmem(4, 3, *tile), vmem(4, 3, *tile), vmem(4, 3, *tile),
            vmem(2, 3, *tile), vmem(2, 3, *tile), vmem(8, 3, *tile),
            vmem(8, 3, *tile), vmem(4, 3, *tile), vmem(4, 3, *tile), vmem(4, 3, *tile), vmem(3, *tile), vmem(2, *tile), vmem(256, 256),
            vmem(8, 16, 256, dtype=F32), vmem(8, 16, 256, dtype=F32), vmem(16, 16, 256),
            vmem(8, 16, 256, dtype=F32), vmem(8, 128, dtype=F32), vmem(8, 8, 128, dtype=F32),
            vmem(2, 192, dtype=jnp.int32), vmem(1, 128, dtype=F32), vmem(384, 128),
            vmem(8, 256, dtype=F32), vmem(2, 8, 256, dtype=jnp.int32),
            pltpu.SMEM((2, 8, 256), jnp.int32),
            pltpu.SemaphoreType.DMA((copies,)), pltpu.SemaphoreType.DMA((copies,)),
            pltpu.SemaphoreType.DMA((11,)),
        ],
        compiler_params=pltpu.CompilerParams(
            collective_id=1, has_side_effects=True, vmem_limit_bytes=LIMIT
        ),
        name="layer",
    )(
        features.reshape(3, 128, 256), weight, bias.reshape(1, 128), coords[0, 0].T, counts[0],
        cotangent, blocks[0, 0],
    )
    outputs, grad_in, grad_w, grad_b = pl.pallas_call(
        emit,
        out_shape=shapes,
        in_specs=[VMEM] * 4,
        out_specs=[VMEM] * 4,
        name="emit",
    )(*results)
    return outputs, grad_in, grad_w, grad_b.reshape(128)


def solution(mesh):
    in_specs = (
        P(("col", "row"), None),
        P(None, "feat"),
        P("feat"),
        P("row", "col", None, None, None),
        P("row", "col", None, None),
        P("row", "col"),
        P(("row", "col"), "feat"),
    )
    out_specs = (
        P(("row", "col"), "feat"),
        P(("col", "row", "feat"), None),
        P(None, "feat"),
        P("feat"),
    )
    return jax.shard_map(body, mesh=mesh, in_specs=in_specs, out_specs=out_specs, check_vma=False)
```

```python
import functools

import jax
import jax.numpy as jnp
from jax import lax
from jax.experimental import pallas as pl
from jax.experimental.pallas import tpu as pltpu
from jax.sharding import PartitionSpec as P

BF = jnp.bfloat16
F32 = jnp.float32
MESH = pl.DeviceIdType.MESH
VMEM = pl.BlockSpec(memory_space=pltpu.VMEM)
SMEM = pl.BlockSpec(memory_space=pltpu.SMEM)
ANY = pl.BlockSpec(memory_space=pl.ANY)
LIMIT = 62 * 1024 * 1024


class Net:
    def __init__(self, send_sems, recv_sems):
        self.send_sems, self.recv_sems, self.copies, self.drained = send_sems, recv_sems, [], 0

    def send(self, src, dst, device):
        index = len(self.copies)
        copy = pltpu.make_async_remote_copy(
            src_ref=src,
            dst_ref=dst,
            send_sem=self.send_sems.at[index],
            recv_sem=self.recv_sems.at[index],
            device_id=device,
            device_id_type=MESH,
        )
        copy.start()
        self.copies.append(copy)
        return copy

    def drain(self, end=None):
        end = len(self.copies) if end is None else end
        for copy in self.copies[self.drained:end]:
            copy.wait_send()
        self.drained = end


def greet(devices):
    barrier = pltpu.get_barrier_semaphore()
    for device in devices:
        pl.semaphore_signal(barrier, inc=1, device_id=device, device_id_type=MESH)
    return lambda: pl.semaphore_wait(barrier, len(devices))


def interleave(streams):
    streams = list(streams)
    while streams:
        alive = []
        for stream in streams:
            try:
                next(stream)
                alive.append(stream)
            except StopIteration:
                pass
        streams = alive


def wrap(index, size):
    return lax.rem(index + 2 * size, size)


def order_slots(coord, count, key, targets, lists, work):
    size, half = 256, 128
    work[0:2, :] = jnp.full((2, size), 63.0, F32)
    work[0:2, 0:192] = coord[...].astype(F32)
    one, zero = jnp.float32(1.0), jnp.float32(0.0)
    lane = lax.broadcasted_iota(jnp.int32, (size, size), 1)
    sub = lax.broadcasted_iota(jnp.int32, (size, size), 0)
    keys = jnp.where(lane[0:1] < count, work[key:key + 1, :], 63.0)
    takes = work[1 - key:2 - key, :]
    key_of = jnp.broadcast_to(keys, (half, size)).T
    wide = jnp.concatenate([key_of, key_of], axis=1)
    same = jnp.where(wide == keys, one, zero)
    rank_row = jnp.sum(jnp.where(sub < lane, same, zero), axis=0, keepdims=True)
    rank = jnp.dot(
        jnp.where(lane < sub, same, zero).astype(BF), jnp.ones((size, half), BF), preferred_element_type=F32
    )
    member = jnp.where(key_of == lane[:, :half].astype(F32), one, zero)
    number = jnp.sum(member, axis=0, keepdims=True)
    number = jnp.where(lane[0:1, :half] < targets, number, zero)
    steps = jnp.floor((number + 1.0) * 0.5)
    lower = jnp.where(sub[:half, :half] < lane[:half, :half], one, zero).astype(BF)
    start = jnp.dot(jnp.broadcast_to(steps, (half, half)).astype(BF), lower, preferred_element_type=F32)
    start_of = lax.dot_general(
        member.astype(BF), start.astype(BF), (((1,), (1,)), ((), ())), preferred_element_type=F32
    )
    place = jnp.where(key_of > 62.0, -1.0, 2.0 * start_of + rank)
    lane_f = lane.astype(F32)
    hit = jnp.where(jnp.concatenate([place, place], axis=1) == lane_f, one, zero).astype(BF)
    kind = sub[0:16]
    opens = jnp.where(rank_row == 0.0, one, zero)
    values = jnp.where(kind == 0, lane_f[0:16] - 192.0, jnp.where(kind == 1, takes, jnp.where(kind == 2, opens, zero)))
    found = jnp.dot(values.astype(BF), hit, preferred_element_type=F32).astype(jnp.int32)
    lists[0:1, :] = jnp.clip(found[0:1] + 192, 0, 192)
    lists[1:2, :] = jnp.clip(found[1:2], 0, 71 - targets)
    lists[2:3, :] = jnp.clip(found[2:3], 0, 1)
    lists[3:4, 0:half] = jnp.clip((start[0:1] + steps - 1.0).astype(jnp.int32), 0, 95 + targets // 2)
    lists[4:5, 0:half] = jnp.where(number > 0.0, 1, 0)


def products(table, blk, src, run_of, steps, unroll, transpose):
    def group(i, run):
        for u in range(unroll):
            q = i * unroll + u
            s0, s1 = table[0, 2 * q], table[0, 2 * q + 1]
            t0, t1 = table[1, 2 * q], table[1, 2 * q + 1]
            if transpose:
                lhs = jnp.concatenate([src[t0], src[t1]], axis=1)
                rhs = jnp.concatenate([blk[s0], blk[s1]], axis=0)
            else:
                lhs = jnp.concatenate([blk[s0], blk[s1]], axis=1)
                rhs = jnp.concatenate([src[t0], src[t1]], axis=0)
            prod = jnp.dot(lhs, rhs, preferred_element_type=F32)
            run = jnp.where(table[2, 2 * q] == 1, 0.0, run) + prod
            run_of[q] = run
        return run

    lax.fori_loop(0, steps // unroll, group, jnp.zeros((128, 128), F32))


def layer(
    feat_ref, w_ref, bias_ref, coord_ref, count_ref, cot_ref, blocks_ref,
    out_ref, gin_ref, gw_ref, gb_ref,
    xw, fall, wfull, blk, run_of, p, g, rp, rm, sp, sm, dp, dm, xr,
    p5, cr, rp5, sp5, g5, h, gin, part5, w1, w2, w3, bsend, brecv,
    coord, bias, cot, work, lists, table, send_sems, recv_sems, local_sems,
):
    row = lax.axis_index("row")
    y, core = row // 2, lax.rem(row, 2)
    col = lax.axis_index("col")
    z, x = col // 2, lax.rem(col, 2)
    f = lax.axis_index("feat")
    sib = {"row": y * 2 + 1 - core}
    yup = {"row": wrap(y + 1, 4) * 2 + core}
    ydown = {"row": wrap(y - 1, 4) * 2 + core}
    yfar = {"row": wrap(y + 2, 4) * 2 + core}
    other = {"feat": 1 - f}
    nbr = {"col": z * 2 + 1 - x}
    up = {"col": wrap(z + 1, 8) * 2 + x}
    down = {"col": wrap(z - 1, 8) * 2 + x}
    up_x = {"col": wrap(z + 1, 8) * 2 + 1 - x}
    down_x = {"col": wrap(z - 1, 8) * 2 + 1 - x}
    rows_of = [{"row": wrap(row + k, 8)} for k in range(1, 8)]
    cols_of = [{"col": wrap(col + k, 16)} for k in range(1, 16)]
    wait = greet(rows_of + cols_of + [other])
    net = Net(send_sems, recv_sems)
    A, B, ALL, THREE = pl.ds(0, 64), pl.ds(64, 64), pl.ds(0, 128), pl.ds(0, 3)

    fetches = []

    def fetch(src, dst):
        copy = pltpu.make_async_copy(src, dst, local_sems.at[len(fetches)])
        copy.start()
        fetches.append(copy)

    fetch(feat_ref, fall.at[row])
    fetch(w_ref, wfull.at[f])
    fetch(coord_ref, coord)
    fetch(bias_ref, bias)
    fetch(cot_ref, cot)
    for n in range(4):
        span = pl.ds(n * 48, 48)
        fetch(blocks_ref.at[span], blk.at[span])
    fetches[0].wait()
    fetches[1].wait()
    own = jnp.dot(fall[row].reshape(384, 256), wfull[f], preferred_element_type=F32).astype(BF)
    xw[row] = own.reshape(3, 128, 128)
    blk[192] = jnp.zeros((128, 128), BF)
    wait()

    def gather_row(buf):
        def move(slot, device, b, rows=ALL):
            ref = buf.at[slot, b, rows]
            return net.send(ref, ref, device)

        lower = wrap(y - 1, 4) * 2 + core
        upper = wrap(y + 1, 4) * 2 + core
        far = wrap(y + 2, 4) * 2 + core
        ups, downs, rest, far_u, far_d = {}, {}, [], {}, {}
        for bu, bd in ((0, 2), (1, 1), (2, 0)):
            ups[bu] = move(row, yup, bu)
            downs[bd] = move(row, ydown, bd)
        for b in range(3):
            rest.append(move(row, sib, b))
        yield
        for bu, bd in ((0, 2), (1, 1), (2, 0)):
            ups[bu].wait_recv()
            if bu < 2:
                far_u[bu] = move(lower, yup, bu, ALL if bu == 0 else A)
            rest.append(move(lower, sib, bu))
            downs[bd].wait_recv()
            if bd > 0:
                far_d[bd] = move(upper, ydown, bd, ALL if bd == 2 else B)
            rest.append(move(upper, sib, bd))
        yield
        for copies, b, rows in ((far_u, 0, ALL), (far_d, 2, ALL), (far_u, 1, A), (far_d, 1, B)):
            copies[b].wait_recv()
            rest.append(move(far, sib, b, rows))
        yield
        for copy in rest:
            copy.wait_recv()

    def order(n, key, targets):
        order_slots(coord, count_ref[0], key, targets, lists.at[n], work)
        fetch(lists.at[n], table.at[n])
        yield

    fetches[2].wait()
    interleave([gather_row(xw), order(0, 0, 48)])
    features_to_all = gather_row(fall)
    next(features_to_all)
    wcopy = net.send(wfull.at[f], wfull.at[f], other)
    for copy in fetches[3:]:
        copy.wait()
    fetches.clear()
    products(table.at[0], blk, xw.reshape(24, 128, 128), run_of, 120, 24, False)

    def summed(n, t):
        return jnp.where(table[n, 4, t] == 1, run_of[table[n, 3, t]], 0.0)

    starts = {}

    def place(k, side):
        shard = wrap(z + k, 8) * 2 + side
        for b in range(3):
            p[shard, b] = summed(0, shard * 3 + b).astype(BF)
        return shard

    shard, cross = place(4, x), place(4, 1 - x)
    for b in range(3):
        starts["u", b] = net.send(p.at[shard, b, A], rp.at[0, b, A], up)
        starts["d", b] = net.send(p.at[shard, b, B], rm.at[0, b, B], down)
        starts["u4", b] = net.send(p.at[cross, b, A], dp.at[0, b, A], up_x)
        starts["d4", b] = net.send(p.at[cross, b, B], dm.at[0, b, B], down_x)
    for name, k, landing, device in (("u3", 3, dp, up_x), ("d3", -3, dm, down_x)):
        shard = place(k, 1 - x)
        for b in range(3):
            starts[name, b] = net.send(p.at[shard, b], landing.at[1, b], device)
    for k in (2, -2, 1, -1, 0):
        shard = place(k, 1 - x)
        for b in range(3):
            starts[k, b] = net.send(p.at[shard, b], xr.at[k % 8, b], nbr)

    def own(k, b):
        return summed(0, (wrap(z + k, 8) * 2 + x) * 3 + b)

    def wide(ref):
        return ref.astype(F32)

    def reduce_col(b):
        u, d = starts["u", b], starts["d", b]
        u.wait_recv()
        starts["u4", b].wait_recv()
        value = own(3, b)
        sp[1, b, A] = (value[:64] + wide(rp[0, b, A]) + wide(dp[0, b, A])).astype(BF)
        sp[1, b, B] = value[64:].astype(BF)
        u = net.send(sp.at[1, b], rp.at[1, b], up)
        d.wait_recv()
        starts["d4", b].wait_recv()
        value = own(-3, b)
        sm[1, b, A] = value[:64].astype(BF)
        sm[1, b, B] = (value[64:] + wide(rm[0, b, B]) + wide(dm[0, b, B])).astype(BF)
        d = net.send(sm.at[1, b], rm.at[1, b], down)
        yield
        for t in (2, 3):
            k = 4 - t
            u.wait_recv()
            starts[k, b].wait_recv()
            value = own(k, b) + wide(xr[k, b]) + wide(rp[t - 1, b])
            if t == 2:
                starts["u3", b].wait_recv()
                value += wide(dp[1, b])
            sp[t, b] = value.astype(BF)
            u = net.send(sp.at[t, b], rp.at[t, b], up)
            d.wait_recv()
            starts[-k, b].wait_recv()
            value = own(-k, b) + wide(xr[8 - k, b]) + wide(rm[t - 1, b])
            if t == 2:
                starts["d3", b].wait_recv()
                value += wide(dm[1, b])
            sm[t, b] = value.astype(BF)
            d = net.send(sm.at[t, b], rm.at[t, b], down)
            yield
        starts[0, b].wait_recv()
        value = own(0, b) + wide(xr[0, b])
        u.wait_recv()
        d.wait_recv()
        return value + wide(rp[3, b]) + wide(rm[3, b])

    def activate(b, total):
        rows = pl.ds(b * 128, 128)
        pre = total + bias[...]
        s = 1.0 / (1.0 + jnp.exp(-pre))
        out_ref[rows] = (pre * s).astype(BF)
        gz = cot[rows].astype(F32) * s * (1.0 + pre * (1.0 - s))
        g[col, b] = gz.T.astype(BF)

    def gather_col(b):
        def move(slot, device, rows=ALL):
            ref = g.at[slot, b, rows]
            return net.send(ref, ref, device)

        rest = []
        last = {1: move(col, up), -1: move(col, down)}
        rest.append(move(col, nbr))
        for hop in range(1, 5):
            yield
            for sign, device, cross, rows in ((1, up, up_x, A), (-1, down, down_x, B)):
                slot = wrap(z - sign * hop, 8) * 2 + x
                last[sign].wait_recv()
                if hop < 4:
                    part = ALL if hop < 3 else rows
                    last[sign] = move(slot, device, part)
                    if hop < 3:
                        if hop == 2:
                            rest.append(move(slot, cross))
                        rest.append(move(slot, nbr))
                    else:
                        rest.append(move(slot, cross, rows))
        yield
        for copy in rest:
            copy.wait_recv()

    def stream(b):
        total = yield from reduce_col(b)
        activate(b, total)
        yield from gather_col(b)

    interleave([stream(0), stream(1), stream(2), order(1, 1, 24), features_to_all])
    fetches[0].wait()

    products(table.at[1], blk, g.reshape(48, 128, 128), run_of, 108, 27, True)

    to_core = {}
    for k in (2, 1, -1, 0):
        shard = wrap(y + k, 4) * 2 + 1 - core
        for b in range(3):
            p5[shard, b] = summed(1, shard * 3 + b).astype(BF)
        to_core[k] = net.send(p5.at[shard], cr.at[k % 4], sib)
    for k in (2, 1, -1, 0):
        shard = wrap(y + k, 4) * 2 + core
        for b in range(3):
            p5[shard, b] = summed(1, shard * 3 + b).astype(BF)

    def mine(k, b, rows):
        slot = wrap(y + k, 4) * 2 + core
        return p5[slot, b, rows].astype(F32) + cr[k % 4, b, rows].astype(F32)

    def input_gradient():
        far = {}
        for b in (1, 0, 2):
            for k, device in ((2, yfar), (1, yup), (-1, ydown)):
                if b == 1:
                    to_core[k].wait_recv()
                sp5[k % 4, b] = mine(k, b, ALL).astype(BF)
                far[k, b] = net.send(sp5.at[k % 4, b], rp5.at[k % 4, b], device)
        yield
        to_core[0].wait_recv()
        halves = []
        for b in (1, 0, 2):
            total = mine(0, b, ALL)
            for k in (1, -1, 2):
                far[k, b].wait_recv()
                total += rp5[k % 4, b].astype(F32)
            g5[b] = total.astype(BF)
            if b == 1:
                halves.append(net.send(g5.at[1], h.at[f], other))
        halves.append(net.send(g5.at[2 - 2 * f], h.at[1 - f], other))
        yield
        wcopy.wait_recv()
        for copy in halves:
            copy.wait_recv()
        for n in range(2):
            block = jnp.dot(wfull[f], g5[f + n], preferred_element_type=F32)
            block += jnp.dot(wfull[1 - f], h[n], preferred_element_type=F32)
            gin[pl.ds(n * 128, 128)] = block.T.astype(BF)
        gin_ref[...] = gin[pl.ds(pl.multiple_of(f * 64, 64), 192)]

    def weight_gradient():
        gwt = jnp.zeros((128, 256), F32)
        for j in range(0, 24, 2):
            a, b = (j // 3, j % 3), ((j + 1) // 3, (j + 1) % 3)
            lhs = jnp.concatenate([p5[a], p5[b]], axis=1)
            rhs = jnp.concatenate([fall[a], fall[b]], axis=0)
            gwt += jnp.dot(lhs, rhs, preferred_element_type=F32)
        for r in range(8):
            part5[r] = gwt[r * 16:(r + 1) * 16].astype(BF)
        copies = []
        for k in range(1, 8):
            copies.append(net.send(part5.at[wrap(row + k, 8)], w1.at[row], rows_of[k - 1]))
        w1[row] = part5[row]
        yield

        def add(t, total):
            return total + g[t // 3, lax.rem(t, 3)].astype(F32)

        nodes = lax.fori_loop(0, 48, add, jnp.zeros((128, 128), F32), unroll=4)
        bsend[...] = jnp.broadcast_to(jnp.sum(nodes.T, axis=0, keepdims=True), (8, 128))
        for copy in copies:
            copy.wait_recv()
        total = w1[0].astype(F32)
        for r in range(1, 8):
            total += w1[r].astype(F32)
        w2[col] = total.astype(BF)
        before = len(net.copies)
        copies = [net.send(w2.at[col], w2.at[col], cols_of[k - 1]) for k in range(1, 16)]
        biases = [net.send(bsend, brecv.at[row], rows_of[k - 1]) for k in range(1, 8)]
        brecv[row] = bsend[...]
        net.drain(before)
        yield
        for copy in copies:
            copy.wait_recv()
        total = w2[0].astype(F32)
        for c in range(1, 16):
            total += w2[c].astype(F32)
        w3[row] = total
        copies = [net.send(w3.at[row], w3.at[row], rows_of[k - 1]) for k in range(1, 8)]
        for copy in biases:
            copy.wait_recv()
        gb_ref[...] = jnp.sum(brecv[...], axis=0)[0:1]
        net.drain(len(net.copies) - 7)
        yield
        for copy in copies:
            copy.wait_recv()
        gw_ref[...] = w3[...].reshape(128, 256).T

    interleave([weight_gradient(), input_gradient()])
    net.drain()


def emit(*refs):
    for n in range(4):
        refs[4 + n][...] = refs[n][...]


def body(features, weight, bias, blocks, coords, counts, cotangent):
    shape = jax.ShapeDtypeStruct
    tile = (128, 128)

    def vmem(*dims, dtype=BF):
        return pltpu.VMEM(dims, dtype)

    copies = 200
    shapes = [
        shape((384, 128), BF), shape((192, 256), BF), shape((256, 128), F32), shape((1, 128), F32),
    ]
    results = pl.pallas_call(
        layer,
        out_shape=shapes,
        in_specs=[ANY, ANY, ANY, ANY, SMEM, ANY, ANY],
        out_specs=[VMEM] * 4,
        scratch_shapes=[
            vmem(8, 3, *tile), vmem(8, 3, 128, 256), vmem(2, 256, 128), vmem(193, *tile),
            vmem(120, *tile, dtype=F32), vmem(16, 3, *tile), vmem(16, 3, *tile),
            vmem(4, 3, *tile), vmem(4, 3, *tile), vmem(4, 3, *tile), vmem(4, 3, *tile),
            vmem(2, 3, *tile), vmem(2, 3, *tile), vmem(8, 3, *tile),
            vmem(8, 3, *tile), vmem(4, 3, *tile), vmem(4, 3, *tile), vmem(4, 3, *tile), vmem(3, *tile), vmem(2, *tile), vmem(256, 256),
            vmem(8, 16, 256), vmem(8, 16, 256), vmem(16, 16, 256),
            vmem(8, 16, 256, dtype=F32), vmem(8, 128, dtype=F32), vmem(8, 8, 128, dtype=F32),
            vmem(2, 192, dtype=jnp.int32), vmem(1, 128, dtype=F32), vmem(384, 128),
            vmem(8, 256, dtype=F32), vmem(2, 8, 256, dtype=jnp.int32),
            pltpu.SMEM((2, 8, 256), jnp.int32),
            pltpu.SemaphoreType.DMA((copies,)), pltpu.SemaphoreType.DMA((copies,)),
            pltpu.SemaphoreType.DMA((11,)),
        ],
        compiler_params=pltpu.CompilerParams(
            collective_id=1, has_side_effects=True, vmem_limit_bytes=LIMIT
        ),
        name="layer",
    )(
        features.reshape(3, 128, 256), weight, bias.reshape(1, 128), coords[0, 0].T, counts[0],
        cotangent, blocks[0, 0],
    )
    outputs, grad_in, grad_w, grad_b = pl.pallas_call(
        emit,
        out_shape=shapes,
        in_specs=[VMEM] * 4,
        out_specs=[VMEM] * 4,
        name="emit",
    )(*results)
    return outputs, grad_in, grad_w, grad_b.reshape(128)


def solution(mesh):
    in_specs = (
        P(("col", "row"), None),
        P(None, "feat"),
        P("feat"),
        P("row", "col", None, None, None),
        P("row", "col", None, None),
        P("row", "col"),
        P(("row", "col"), "feat"),
    )
    out_specs = (
        P(("row", "col"), "feat"),
        P(("col", "row", "feat"), None),
        P(None, "feat"),
        P("feat"),
    )
    return jax.shard_map(body, mesh=mesh, in_specs=in_specs, out_specs=out_specs, check_vma=False)
```

```python
import functools

import jax
import jax.numpy as jnp
from jax import lax
from jax.experimental import pallas as pl
from jax.experimental.pallas import tpu as pltpu
from jax.sharding import PartitionSpec as P

BF = jnp.bfloat16
F32 = jnp.float32
MESH = pl.DeviceIdType.MESH
VMEM = pl.BlockSpec(memory_space=pltpu.VMEM)
SMEM = pl.BlockSpec(memory_space=pltpu.SMEM)
ANY = pl.BlockSpec(memory_space=pl.ANY)
LIMIT = 62 * 1024 * 1024


class Net:
    def __init__(self, send_sems, recv_sems):
        self.send_sems, self.recv_sems, self.copies, self.drained = send_sems, recv_sems, [], 0

    def send(self, src, dst, device):
        index = len(self.copies)
        copy = pltpu.make_async_remote_copy(
            src_ref=src,
            dst_ref=dst,
            send_sem=self.send_sems.at[index],
            recv_sem=self.recv_sems.at[index],
            device_id=device,
            device_id_type=MESH,
        )
        copy.start()
        self.copies.append(copy)
        return copy

    def drain(self, end=None):
        end = len(self.copies) if end is None else end
        for copy in self.copies[self.drained:end]:
            copy.wait_send()
        self.drained = end


def greet(devices):
    barrier = pltpu.get_barrier_semaphore()
    for device in devices:
        pl.semaphore_signal(barrier, inc=1, device_id=device, device_id_type=MESH)
    return lambda: pl.semaphore_wait(barrier, len(devices))


def interleave(streams):
    streams = list(streams)
    while streams:
        alive = []
        for stream in streams:
            try:
                next(stream)
                alive.append(stream)
            except StopIteration:
                pass
        streams = alive


def wrap(index, size):
    return lax.rem(index + 2 * size, size)


def order_slots(coord, count, key, targets, lists, work):
    size, half = 256, 128
    work[0:2, :] = jnp.full((2, size), 63.0, F32)
    work[0:2, 0:192] = coord[...].astype(F32)
    one, zero = jnp.float32(1.0), jnp.float32(0.0)
    lane = lax.broadcasted_iota(jnp.int32, (size, size), 1)
    sub = lax.broadcasted_iota(jnp.int32, (size, size), 0)
    keys = jnp.where(lane[0:1] < count, work[key:key + 1, :], 63.0)
    takes = work[1 - key:2 - key, :]
    key_of = jnp.broadcast_to(keys, (half, size)).T
    wide = jnp.concatenate([key_of, key_of], axis=1)
    same = jnp.where(wide == keys, one, zero)
    rank_row = jnp.sum(jnp.where(sub < lane, same, zero), axis=0, keepdims=True)
    rank = jnp.dot(
        jnp.where(lane < sub, same, zero).astype(BF), jnp.ones((size, half), BF), preferred_element_type=F32
    )
    member = jnp.where(key_of == lane[:, :half].astype(F32), one, zero)
    number = jnp.sum(member, axis=0, keepdims=True)
    number = jnp.where(lane[0:1, :half] < targets, number, zero)
    steps = jnp.floor((number + 1.0) * 0.5)
    lower = jnp.where(sub[:half, :half] < lane[:half, :half], one, zero).astype(BF)
    start = jnp.dot(jnp.broadcast_to(steps, (half, half)).astype(BF), lower, preferred_element_type=F32)
    start_of = lax.dot_general(
        member.astype(BF), start.astype(BF), (((1,), (1,)), ((), ())), preferred_element_type=F32
    )
    place = jnp.where(key_of > 62.0, -1.0, 2.0 * start_of + rank)
    lane_f = lane.astype(F32)
    hit = jnp.where(jnp.concatenate([place, place], axis=1) == lane_f, one, zero).astype(BF)
    kind = sub[0:16]
    opens = jnp.where(rank_row == 0.0, one, zero)
    values = jnp.where(kind == 0, lane_f[0:16] - 192.0, jnp.where(kind == 1, takes, jnp.where(kind == 2, opens, zero)))
    found = jnp.dot(values.astype(BF), hit, preferred_element_type=F32).astype(jnp.int32)
    lists[0:1, :] = jnp.clip(found[0:1] + 192, 0, 192)
    lists[1:2, :] = jnp.clip(found[1:2], 0, 71 - targets)
    lists[2:3, :] = jnp.clip(found[2:3], 0, 1)
    lists[3:4, 0:half] = jnp.clip((start[0:1] + steps - 1.0).astype(jnp.int32), 0, 95 + targets // 2)
    lists[4:5, 0:half] = jnp.where(number > 0.0, 1, 0)


def products(table, blk, src, run_of, steps, unroll, transpose):
    def group(i, run):
        for u in range(unroll):
            q = i * unroll + u
            s0, s1 = table[0, 2 * q], table[0, 2 * q + 1]
            t0, t1 = table[1, 2 * q], table[1, 2 * q + 1]
            if transpose:
                lhs = jnp.concatenate([src[t0], src[t1]], axis=1)
                rhs = jnp.concatenate([blk[s0], blk[s1]], axis=0)
            else:
                lhs = jnp.concatenate([blk[s0], blk[s1]], axis=1)
                rhs = jnp.concatenate([src[t0], src[t1]], axis=0)
            prod = jnp.dot(lhs, rhs, preferred_element_type=F32)
            run = jnp.where(table[2, 2 * q] == 1, 0.0, run) + prod
            run_of[q] = run
        return run

    lax.fori_loop(0, steps // unroll, group, jnp.zeros((128, 128), F32))


def layer(
    feat_ref, w_ref, bias_ref, coord_ref, count_ref, cot_ref, blocks_ref,
    out_ref, gin_ref, gw_ref, gb_ref,
    xw, fall, wfull, blk, run_of, p, g, rp, rm, sp, sm, dp, dm, xr,
    p5, cr, rp5, sp5, g5, h, gin, part5, w1, w2, w3, bsend, brecv,
    wide_of, agg, carry,
    coord, bias, cot, work, lists, table, send_sems, recv_sems, local_sems,
):
    row = lax.axis_index("row")
    y, core = row // 2, lax.rem(row, 2)
    col = lax.axis_index("col")
    z, x = col // 2, lax.rem(col, 2)
    f = lax.axis_index("feat")
    sib = {"row": y * 2 + 1 - core}
    yup = {"row": wrap(y + 1, 4) * 2 + core}
    ydown = {"row": wrap(y - 1, 4) * 2 + core}
    yfar = {"row": wrap(y + 2, 4) * 2 + core}
    other = {"feat": 1 - f}
    nbr = {"col": z * 2 + 1 - x}
    up = {"col": wrap(z + 1, 8) * 2 + x}
    down = {"col": wrap(z - 1, 8) * 2 + x}
    up_x = {"col": wrap(z + 1, 8) * 2 + 1 - x}
    down_x = {"col": wrap(z - 1, 8) * 2 + 1 - x}
    rows_of = [{"row": wrap(row + k, 8)} for k in range(1, 8)]
    cols_of = [{"col": wrap(col + k, 16)} for k in range(1, 16)]
    wait = greet(rows_of + cols_of + [other])
    net = Net(send_sems, recv_sems)
    A, B, ALL, THREE = pl.ds(0, 64), pl.ds(64, 64), pl.ds(0, 128), pl.ds(0, 3)

    fetches = []

    def fetch(src, dst):
        copy = pltpu.make_async_copy(src, dst, local_sems.at[len(fetches)])
        copy.start()
        fetches.append(copy)

    fetch(feat_ref, fall.at[row])
    fetch(w_ref, wfull.at[f])
    fetch(coord_ref, coord)
    fetch(bias_ref, bias)
    fetch(cot_ref, cot)
    for n in range(4):
        span = pl.ds(n * 48, 48)
        fetch(blocks_ref.at[span], blk.at[span])
    fetches[0].wait()
    fetches[1].wait()
    own = jnp.dot(fall[row].reshape(384, 256), wfull[f], preferred_element_type=F32).astype(BF)
    xw[row] = own.reshape(3, 128, 128)
    blk[192] = jnp.zeros((128, 128), BF)
    wait()

    def gather_row(buf):
        def move(slot, device, b, rows=ALL):
            ref = buf.at[slot, b, rows]
            return net.send(ref, ref, device)

        lower = wrap(y - 1, 4) * 2 + core
        upper = wrap(y + 1, 4) * 2 + core
        far = wrap(y + 2, 4) * 2 + core
        ups, downs, rest, far_u, far_d = {}, {}, [], {}, {}
        for bu, bd in ((0, 2), (1, 1), (2, 0)):
            ups[bu] = move(row, yup, bu)
            downs[bd] = move(row, ydown, bd)
        for b in range(3):
            rest.append(move(row, sib, b))
        yield
        for bu, bd in ((0, 2), (1, 1), (2, 0)):
            ups[bu].wait_recv()
            if bu < 2:
                far_u[bu] = move(lower, yup, bu, ALL if bu == 0 else A)
            rest.append(move(lower, sib, bu))
            downs[bd].wait_recv()
            if bd > 0:
                far_d[bd] = move(upper, ydown, bd, ALL if bd == 2 else B)
            rest.append(move(upper, sib, bd))
        yield
        for copies, b, rows in ((far_u, 0, ALL), (far_d, 2, ALL), (far_u, 1, A), (far_d, 1, B)):
            copies[b].wait_recv()
            rest.append(move(far, sib, b, rows))
        yield
        for copy in rest:
            copy.wait_recv()

    def gather_row_direct(buf):
        def move(slot, device):
            ref = buf.at[slot]
            return net.send(ref, ref, device)

        far, upper, lower = move(row, yfar), move(row, yup), move(row, ydown)
        rest = [move(row, sib)]
        yield
        for copy, k in ((upper, -1), (lower, 1), (far, 2)):
            copy.wait_recv()
            rest.append(move(wrap(y + k, 4) * 2 + core, sib))
        yield
        for copy in rest:
            copy.wait_recv()

    def order(n, key, targets):
        order_slots(coord, count_ref[0], key, targets, lists.at[n], work)
        fetch(lists.at[n], table.at[n])
        yield

    fetches[2].wait()
    interleave([gather_row(xw), order(0, 0, 48)])
    features_to_all = gather_row_direct(fall)
    next(features_to_all)
    wcopy = net.send(wfull.at[f], wfull.at[f], other)
    for copy in fetches[3:]:
        copy.wait()
    fetches.clear()
    products(table.at[0], blk, xw.reshape(24, 128, 128), run_of, 120, 24, False)

    def summed(n, t):
        return jnp.where(table[n, 4, t] == 1, run_of[table[n, 3, t]], 0.0)

    starts = {}

    def place(k, side):
        shard = wrap(z + k, 8) * 2 + side
        for b in range(3):
            p[shard, b] = summed(0, shard * 3 + b).astype(BF)
        return shard

    shard, cross = place(4, x), place(4, 1 - x)
    for b in range(3):
        starts["u", b] = net.send(p.at[shard, b, A], rp.at[0, b, A], up)
        starts["d", b] = net.send(p.at[shard, b, B], rm.at[0, b, B], down)
        starts["u4", b] = net.send(p.at[cross, b, A], dp.at[0, b, A], up_x)
        starts["d4", b] = net.send(p.at[cross, b, B], dm.at[0, b, B], down_x)
    for name, k, landing, device in (("u3", 3, dp, up_x), ("d3", -3, dm, down_x)):
        shard = place(k, 1 - x)
        for b in range(3):
            starts[name, b] = net.send(p.at[shard, b], landing.at[1, b], device)
    for k in (2, -2, 1, -1, 0):
        shard = place(k, 1 - x)
        for b in range(3):
            starts[k, b] = net.send(p.at[shard, b], xr.at[k % 8, b], nbr)

    def own(k, b):
        return summed(0, (wrap(z + k, 8) * 2 + x) * 3 + b)

    def wide(ref):
        return ref.astype(F32)

    def reduce_col(b):
        u, d = starts["u", b], starts["d", b]
        u.wait_recv()
        starts["u4", b].wait_recv()
        value = own(3, b)
        sp[1, b, A] = (value[:64] + wide(rp[0, b, A]) + wide(dp[0, b, A])).astype(BF)
        sp[1, b, B] = value[64:].astype(BF)
        u = net.send(sp.at[1, b], rp.at[1, b], up)
        d.wait_recv()
        starts["d4", b].wait_recv()
        value = own(-3, b)
        sm[1, b, A] = value[:64].astype(BF)
        sm[1, b, B] = (value[64:] + wide(rm[0, b, B]) + wide(dm[0, b, B])).astype(BF)
        d = net.send(sm.at[1, b], rm.at[1, b], down)
        yield
        for t in (2, 3):
            k = 4 - t
            u.wait_recv()
            starts[k, b].wait_recv()
            value = own(k, b) + wide(xr[k, b]) + wide(rp[t - 1, b])
            if t == 2:
                starts["u3", b].wait_recv()
                value += wide(dp[1, b])
            sp[t, b] = value.astype(BF)
            u = net.send(sp.at[t, b], rp.at[t, b], up)
            d.wait_recv()
            starts[-k, b].wait_recv()
            value = own(-k, b) + wide(xr[8 - k, b]) + wide(rm[t - 1, b])
            if t == 2:
                starts["d3", b].wait_recv()
                value += wide(dm[1, b])
            sm[t, b] = value.astype(BF)
            d = net.send(sm.at[t, b], rm.at[t, b], down)
            yield
        starts[0, b].wait_recv()
        value = own(0, b) + wide(xr[0, b])
        u.wait_recv()
        d.wait_recv()
        return value + wide(rp[3, b]) + wide(rm[3, b])

    def activate(b, total):
        rows = pl.ds(b * 128, 128)
        pre = total + bias[...]
        s = 1.0 / (1.0 + jnp.exp(-pre))
        out_ref[rows] = (pre * s).astype(BF)
        gz = cot[rows].astype(F32) * s * (1.0 + pre * (1.0 - s))
        g[col, b] = gz.T.astype(BF)

    def gather_col(b):
        def move(slot, device, rows=ALL):
            ref = g.at[slot, b, rows]
            return net.send(ref, ref, device)

        rest = []
        last = {1: move(col, up), -1: move(col, down)}
        rest.append(move(col, nbr))
        for hop in range(1, 5):
            yield
            for sign, device, cross, rows in ((1, up, up_x, A), (-1, down, down_x, B)):
                slot = wrap(z - sign * hop, 8) * 2 + x
                last[sign].wait_recv()
                if hop < 4:
                    part = ALL if hop < 3 else rows
                    last[sign] = move(slot, device, part)
                    if hop < 3:
                        if hop == 2:
                            rest.append(move(slot, cross))
                        rest.append(move(slot, nbr))
                    else:
                        rest.append(move(slot, cross, rows))
        yield
        for copy in rest:
            copy.wait_recv()

    def stream(b):
        total = yield from reduce_col(b)
        activate(b, total)
        yield from gather_col(b)

    def aggregate():
        fa = fall.reshape(24, 128, 256)
        for _ in features_to_all:
            pass
        carry[...] = jnp.zeros((128, 256), F32)

        def group(i, run):
            for u in range(10):
                q = i * 10 + u
                s0, s1 = table[0, 0, 2 * q], table[0, 0, 2 * q + 1]
                t0, t1 = table[0, 1, 2 * q], table[0, 1, 2 * q + 1]
                lhs = jnp.concatenate([blk[s0], blk[s1]], axis=1)
                rhs = jnp.concatenate([fa[t0], fa[t1]], axis=0)
                prod = jnp.dot(lhs, rhs, preferred_element_type=F32)
                run = jnp.where(table[0, 2, 2 * q] == 1, 0.0, run) + prod
                wide_of[q] = run
            return run

        for piece in range(6):
            carry[...] = lax.fori_loop(piece * 2, piece * 2 + 2, group, carry[...])
            yield

        def pick(t, c):
            value = wide_of[table[0, 3, t]]
            agg[t] = jnp.where(table[0, 4, t] == 1, value, 0.0).astype(BF)
            return c

        for piece in range(2):
            lax.fori_loop(piece * 24, piece * 24 + 24, pick, 0, unroll=4)
            yield

    next(features_to_all)
    interleave([stream(0), stream(1), stream(2), order(1, 1, 24), aggregate()])
    fetches[0].wait()

    def weight_gradient():
        gwt = jnp.zeros((128, 256), F32)
        gt = g.reshape(48, 128, 128)
        for j in range(0, 48, 2):
            lhs = jnp.concatenate([gt[j], gt[j + 1]], axis=1)
            rhs = jnp.concatenate([agg[j], agg[j + 1]], axis=0)
            gwt += jnp.dot(lhs, rhs, preferred_element_type=F32)
        for r in range(8):
            part5[r] = gwt[r * 16:(r + 1) * 16].astype(BF)
        copies = []
        for k in range(1, 8):
            copies.append(net.send(part5.at[wrap(row + k, 8)], w1.at[row], rows_of[k - 1]))
        w1[row] = part5[row]
        yield

        def add(t, total):
            return total + g[t // 3, lax.rem(t, 3)].astype(F32)

        nodes = lax.fori_loop(0, 48, add, jnp.zeros((128, 128), F32), unroll=4)
        bsend[...] = jnp.broadcast_to(jnp.sum(nodes.T, axis=0, keepdims=True), (8, 128))
        for copy in copies:
            copy.wait_recv()
        total = w1[0].astype(F32)
        for r in range(1, 8):
            total += w1[r].astype(F32)
        w2[col] = total.astype(BF)
        before = len(net.copies)
        copies = [net.send(w2.at[col], w2.at[col], cols_of[k - 1]) for k in range(1, 16)]
        biases = [net.send(bsend, brecv.at[row], rows_of[k - 1]) for k in range(1, 8)]
        brecv[row] = bsend[...]
        net.drain(before)
        yield
        for copy in copies:
            copy.wait_recv()
        total = w2[0].astype(F32)
        for c in range(1, 16):
            total += w2[c].astype(F32)
        w3[row] = total
        copies = [net.send(w3.at[row], w3.at[row], rows_of[k - 1]) for k in range(1, 8)]
        for copy in biases:
            copy.wait_recv()
        gb_ref[...] = jnp.sum(brecv[...], axis=0)[0:1]
        net.drain(len(net.copies) - 7)
        yield
        for copy in copies:
            copy.wait_recv()
        gw_ref[...] = w3[...].reshape(128, 256).T

    weight_stream = weight_gradient()
    next(weight_stream)
    products(table.at[1], blk, g.reshape(48, 128, 128), run_of, 108, 27, True)

    to_core = {}
    for k in (2, 1, -1, 0):
        shard = wrap(y + k, 4) * 2 + 1 - core
        for b in range(3):
            p5[shard, b] = summed(1, shard * 3 + b).astype(BF)
        to_core[k] = net.send(p5.at[shard], cr.at[k % 4], sib)
    for k in (2, 1, -1, 0):
        shard = wrap(y + k, 4) * 2 + core
        for b in range(3):
            p5[shard, b] = summed(1, shard * 3 + b).astype(BF)

    def mine(k, b, rows):
        slot = wrap(y + k, 4) * 2 + core
        return p5[slot, b, rows].astype(F32) + cr[k % 4, b, rows].astype(F32)

    def input_gradient():
        far = {}
        for b in (1, 0, 2):
            for k, device in ((2, yfar), (1, yup), (-1, ydown)):
                if b == 1:
                    to_core[k].wait_recv()
                sp5[k % 4, b] = mine(k, b, ALL).astype(BF)
                far[k, b] = net.send(sp5.at[k % 4, b], rp5.at[k % 4, b], device)
        yield
        to_core[0].wait_recv()
        halves = []
        for b in (1, 0, 2):
            total = mine(0, b, ALL)
            for k in (1, -1, 2):
                far[k, b].wait_recv()
                total += rp5[k % 4, b].astype(F32)
            g5[b] = total.astype(BF)
            if b == 1:
                halves.append(net.send(g5.at[1], h.at[f], other))
        halves.append(net.send(g5.at[2 - 2 * f], h.at[1 - f], other))
        yield
        wcopy.wait_recv()
        for copy in halves:
            copy.wait_recv()
        for n in range(2):
            block = jnp.dot(wfull[f], g5[f + n], preferred_element_type=F32)
            block += jnp.dot(wfull[1 - f], h[n], preferred_element_type=F32)
            gin[pl.ds(n * 128, 128)] = block.T.astype(BF)
        gin_ref[...] = gin[pl.ds(pl.multiple_of(f * 64, 64), 192)]

    interleave([input_gradient(), weight_stream])
    net.drain()


def emit(*refs):
    for n in range(4):
        refs[4 + n][...] = refs[n][...]


def body(features, weight, bias, blocks, coords, counts, cotangent):
    shape = jax.ShapeDtypeStruct
    tile = (128, 128)

    def vmem(*dims, dtype=BF):
        return pltpu.VMEM(dims, dtype)

    copies = 200
    shapes = [
        shape((384, 128), BF), shape((192, 256), BF), shape((256, 128), F32), shape((1, 128), F32),
    ]
    results = pl.pallas_call(
        layer,
        out_shape=shapes,
        in_specs=[ANY, ANY, ANY, ANY, SMEM, ANY, ANY],
        out_specs=[VMEM] * 4,
        scratch_shapes=[
            vmem(8, 3, *tile), vmem(8, 3, 128, 256), vmem(2, 256, 128), vmem(193, *tile),
            vmem(120, *tile, dtype=F32), vmem(16, 3, *tile), vmem(16, 3, *tile),
            vmem(4, 3, *tile), vmem(4, 3, *tile), vmem(4, 3, *tile), vmem(4, 3, *tile),
            vmem(2, 3, *tile), vmem(2, 3, *tile), vmem(8, 3, *tile),
            vmem(8, 3, *tile), vmem(4, 3, *tile), vmem(4, 3, *tile), vmem(4, 3, *tile), vmem(3, *tile), vmem(2, *tile), vmem(256, 256),
            vmem(8, 16, 256), vmem(8, 16, 256), vmem(16, 16, 256),
            vmem(8, 16, 256, dtype=F32), vmem(8, 128, dtype=F32), vmem(8, 8, 128, dtype=F32),
            vmem(120, 128, 256, dtype=F32), vmem(48, 128, 256), vmem(128, 256, dtype=F32),
            vmem(2, 192, dtype=jnp.int32), vmem(1, 128, dtype=F32), vmem(384, 128),
            vmem(8, 256, dtype=F32), vmem(2, 8, 256, dtype=jnp.int32),
            pltpu.SMEM((2, 8, 256), jnp.int32),
            pltpu.SemaphoreType.DMA((copies,)), pltpu.SemaphoreType.DMA((copies,)),
            pltpu.SemaphoreType.DMA((11,)),
        ],
        compiler_params=pltpu.CompilerParams(
            collective_id=1, has_side_effects=True, vmem_limit_bytes=LIMIT
        ),
        name="layer",
    )(
        features.reshape(3, 128, 256), weight, bias.reshape(1, 128), coords[0, 0].T, counts[0],
        cotangent, blocks[0, 0],
    )
    outputs, grad_in, grad_w, grad_b = pl.pallas_call(
        emit,
        out_shape=shapes,
        in_specs=[VMEM] * 4,
        out_specs=[VMEM] * 4,
        name="emit",
    )(*results)
    return outputs, grad_in, grad_w, grad_b.reshape(128)


def solution(mesh):
    in_specs = (
        P(("col", "row"), None),
        P(None, "feat"),
        P("feat"),
        P("row", "col", None, None, None),
        P("row", "col", None, None),
        P("row", "col"),
        P(("row", "col"), "feat"),
    )
    out_specs = (
        P(("row", "col"), "feat"),
        P(("col", "row", "feat"), None),
        P(None, "feat"),
        P("feat"),
    )
    return jax.shard_map(body, mesh=mesh, in_specs=in_specs, out_specs=out_specs, check_vma=False)
```
